32 devices in a mesh: parts: 2 (over x), chol: 16 (over z, y, core).
Axes of the slice: x: 2, y: 2, z: 4, core: 2. Of those that a mesh axis runs over, the one named last changes fastest.
Arguments:
- walkers: bfloat16 [32, 2304, 320], P(('parts', 'chol')), parts along dimension 0, may hold values from -6 to 6
- left_factor: bfloat16 [32, 320, 2304], P(('parts', 'chol')), parts along dimension 0, may hold values from -0.3125 to 0.3125
- chol_tiles: bfloat16 [64, 48, 16384], P('chol'), may hold values from -0.046875 to 0.046875
- tile_block: int32 [64], replicated, may hold values from 0 to 323
- fields: float32 [32, 3072], P('parts', 'chol'), parts along dimension 0, may hold values from -6 to 6
Outputs:
- force_bias: float32 [32, 3072], P('parts', 'chol'), parts along dimension 0
- new_walkers: bfloat16 [32, 2304, 320], P(('parts', 'chol')), parts along dimension 0
The draws below stay inside these ranges and needn't reach their ends.
There are 2 independent parts, one for each index of `parts`. The reference program is written for one: setup_inputs(seed, part) draws one part's arguments, and reference() takes and returns one part's arrays. A program takes and returns all parts, laid end to end along the dimension named above; an argument that names none is the same for every part. Nothing has to cross between parts.
All inputs are finite; a program needn't handle non-finite values.
Results may differ from the reference program's by a relative error of at most 0.0051.
Values may be sent and summed in bfloat16 or wider, within the bound.
A program may use at most 128 MiB of HBM per device.

```python
import jax
import jax.numpy as jnp
from jax import lax

M = 2304
NEL = 320
BS = 128
GT = 48
W = 16
NT = 64
NPAIR = 324
VECTORS = 3072


def with_ends(values, key, low, largest):
    spot = [jax.random.randint(jax.random.fold_in(key, axis), (), 0, length) for axis, length in enumerate(values.shape)]
    widest = values.shape.index(max(values.shape))
    beside = spot[:widest] + [(spot[widest] + 1) % values.shape[widest]] + spot[widest + 1:]
    return values.at[tuple(spot)].set(low).at[tuple(beside)].set(largest)


def levels(stream_key, extent, pieces, smallest, largest):
    factor_of, own = 1.0, jax.random.fold_in(stream_key, 6)
    for position, blocks in pieces:
        steps = jnp.exp(jax.random.uniform(jax.random.fold_in(own, position), (blocks,), jnp.float32, smallest / len(pieces), largest / len(pieces)))
        factor_of = factor_of * jnp.repeat(steps, extent[position] // blocks).reshape([-1 if axis == position else 1 for axis in range(len(extent))])
    return factor_of


def centred(stream_key, shape, width, most, pieces=(), dtype=jnp.bfloat16):
    array = jax.random.normal(stream_key, shape, jnp.float32) * width
    if len(pieces) > 0:
        array = levels(stream_key, shape, pieces, -0.22, 0.18) * array
    return jnp.clip(array, min=-most, max=most).astype(dtype)


def setup_inputs(seed: int = 0, part: int = 0) -> dict:
    streams_of = jax.random.split(jax.random.key(seed), 6)
    own_keys = jax.random.split(jax.random.fold_in(streams_of[5], part), 6)
    walkers = centred(own_keys[0], (W, M, NEL), 1.0, 6.0, ((0, 16),))
    left_factor = centred(own_keys[1], (W, NEL, M), NEL ** -0.5, 0.3125, ((0, 16),))
    chol_tiles = centred(streams_of[2], (NT, GT, BS * BS), (BS * BS) ** -0.5, 0.046875, ((0, 16),))
    tile_block = with_ends(jax.random.randint(streams_of[3], (NT,), 0, NPAIR), jax.random.fold_in(streams_of[3], 1), 0, NPAIR - 1).astype(jnp.int32)
    fields = centred(own_keys[4], (W, VECTORS), 1.0, 6.0, ((1, 16),), jnp.float32)
    return {"walkers": walkers, "left_factor": left_factor, "chol_tiles": chol_tiles, "tile_block": tile_block, "fields": fields}


step_root = 0.25


def reference(walkers, left_factor, chol_tiles, tile_block, fields):
    blocks_side = M // BS
    row_block = tile_block // blocks_side
    col_block = tile_block % blocks_side
    chol_wide = chol_tiles.astype(jnp.float32)
    count = chol_tiles.shape[0]

    def one_walker(items):
        orbitals, factor, field_row = items
        rows = orbitals.reshape(blocks_side, BS, NEL)[row_block].astype(jnp.float32)
        cols = factor.reshape(NEL, blocks_side, BS)[:, col_block].astype(jnp.float32)
        green = jnp.einsum("tie,etk->tik", rows, cols).astype(jnp.bfloat16).reshape(count, BS * BS)
        bias = jnp.einsum("te,tge->tg", green.astype(jnp.float32), chol_wide)
        shifted = (field_row.reshape(count, GT) + bias).astype(jnp.bfloat16)
        parts = jnp.einsum("tg,tge->te", shifted.astype(jnp.float32), chol_wide).astype(jnp.bfloat16)
        summed = jnp.zeros((blocks_side * blocks_side, BS * BS), jnp.float32).at[tile_block].add(parts.astype(jnp.float32))
        whole = summed.reshape(blocks_side, blocks_side, BS, BS).transpose(0, 2, 1, 3).reshape(M, M)
        operator = (-step_root * whole).astype(jnp.bfloat16)
        term = orbitals
        total = orbitals.astype(jnp.float32)
        for order in range(1, 4):
            term = (jnp.dot(operator, term, preferred_element_type=jnp.float32) / order).astype(jnp.bfloat16)
            total = total + term.astype(jnp.float32)
        return bias.reshape(-1), total.astype(jnp.bfloat16)

    force_bias, new_walkers = lax.map(one_walker, (walkers, left_factor, fields))
    return force_bias, new_walkers
```

```python
import functools

import jax
import jax.numpy as jnp
from jax import lax
from jax.experimental import pallas as pl
from jax.experimental.pallas import tpu as pltpu
from jax.sharding import PartitionSpec as P

BS = 128
MESH = pl.DeviceIdType.MESH

step_root = 0.25
CHUNK = 2048


def exchange_kernel(
    n,
    green,
    fields,
    chol_hbm,
    bias_out,
    returned,
    chol,
    received,
    back,
    wide,
    flat,
    field_tiles,
    bias_tiles,
    chol_sem,
    green_send,
    green_recv,
    back_send,
    back_recv,
    own_sem,
):
    me = lax.axis_index("chol")
    part = lax.axis_index("parts")
    tiles, vectors, area = chol.shape
    half = n // 2

    chol_copies = [
        pltpu.make_async_copy(chol_hbm.at[j], chol.at[j], chol_sem.at[j]) for j in range(tiles)
    ]
    for copy in chol_copies:
        copy.start()

    barrier = pltpu.get_barrier_semaphore()

    def greet(r, carry):
        pl.semaphore_signal(
            barrier, inc=1, device_id=(part, lax.rem(me + r, n)), device_id_type=MESH
        )
        return carry

    lax.fori_loop(1, n, greet, 0)

    for j in range(tiles):
        field_tiles[j] = fields[:, j * vectors : (j + 1) * vectors]

    def send_green(j, owner):
        t = owner * tiles + j
        pltpu.make_async_remote_copy(
            src_ref=green.at[t],
            dst_ref=received.at[j, me],
            send_sem=green_send,
            recv_sem=green_recv.at[j],
            device_id=(part, owner),
            device_id_type=MESH,
        ).start()

    for j in range(tiles):
        received[j, me] = green[me * tiles + j]
    pl.semaphore_wait(barrier, n - 1)

    def send_tile(j, carry):
        send_green(j, lax.rem(me + half, n))

        def pair(i, c):
            send_green(j, lax.rem(me + half + i, n))
            send_green(j, lax.rem(me + i, n))
            return c

        return lax.fori_loop(1, half, pair, carry)

    lax.fori_loop(0, tiles, send_tile, 0)

    def send_back(j, walker):
        pltpu.make_async_remote_copy(
            src_ref=back.at[j, walker],
            dst_ref=returned.at[me * tiles + j],
            send_sem=back_send,
            recv_sem=back_recv,
            device_id=(part, walker),
            device_id_type=MESH,
        ).start()

    def process(j, carry):
        arrived = received.at[j, pl.ds(0, n - 1)]
        pltpu.make_async_copy(arrived, arrived, green_recv.at[j]).wait()
        pltpu.make_async_copy(chol_hbm.at[j], chol.at[j], chol_sem.at[j]).wait()
        for w in range(n):
            wide[pl.ds(w, BS, stride=n), :] = received[j, w].astype(jnp.float32)
        for i in range(BS):
            flat[:, i * BS : (i + 1) * BS] = wide[i * n : (i + 1) * n, :].astype(jnp.bfloat16)

        bias = jnp.zeros((n, vectors), jnp.float32)
        for c in range(area // CHUNK):
            bias = bias + lax.dot_general(
                flat[:, c * CHUNK : (c + 1) * CHUNK],
                chol[j, :, c * CHUNK : (c + 1) * CHUNK],
                (((1,), (1,)), ((), ())),
                preferred_element_type=jnp.float32,
            )
        bias_tiles[j] = bias
        shifted = (field_tiles[j] + bias).astype(jnp.bfloat16)
        for c in range(area // CHUNK):
            piece = jnp.dot(
                shifted,
                chol[j, :, c * CHUNK : (c + 1) * CHUNK],
                preferred_element_type=jnp.float32,
            )
            for i in range(CHUNK // BS):
                base = (c * (CHUNK // BS) + i) * n
                wide[base : base + n, :] = piece[:, i * BS : (i + 1) * BS]
        for w in range(n):
            back[j, w] = wide[pl.ds(w, BS, stride=n), :].astype(jnp.bfloat16)

        send_back(j, lax.rem(me + half, n))

        def pair(i, c):
            send_back(j, lax.rem(me + half + i, n))
            send_back(j, lax.rem(me + i, n))
            return c

        lax.fori_loop(1, half, pair, 0)
        pltpu.make_async_copy(
            back.at[j, me], returned.at[me * tiles + j], own_sem.at[j]
        ).start()
        return carry

    lax.fori_loop(0, tiles, process, 0)

    for j in range(tiles):
        bias_out[:, j * vectors : (j + 1) * vectors] = bias_tiles[j]

    others = pl.ds(0, (n - 1) * tiles)
    pltpu.make_async_copy(green.at[others], green.at[others], green_send).wait()
    pltpu.make_async_copy(green.at[others], green.at[others], back_send).wait()
    for j in range(tiles):
        pltpu.make_async_copy(
            back.at[j, me], returned.at[me * tiles + j], own_sem.at[j]
        ).wait()
    pltpu.make_async_copy(returned.at[others], returned.at[others], back_recv).wait()


def build_kernel(group, tile_block, walkers, left_factor, green, rows):
    count = green.shape[0]
    side = rows.shape[0]
    for r in range(side):
        rows[r] = walkers[0, :, r * BS : (r + 1) * BS].T

    def step(s, carry):
        for u in range(group):
            t = s * group + u
            block = tile_block[t]
            row = lax.div(block, side)
            col = block - row * side
            cols = left_factor[0, :, pl.ds(pl.multiple_of(col * BS, BS), BS)]
            green[t] = jnp.dot(rows[row], cols, preferred_element_type=jnp.float32).astype(
                jnp.bfloat16
            )
        return carry

    lax.fori_loop(0, count // group, step, 0)


def propagate_kernel(group, tile_block, parts, walkers, out, term, acc, total):
    count = parts.shape[0]
    side = walkers.shape[2] // BS
    term[...] = walkers[0]
    total[...] = walkers[0].astype(jnp.float32)
    for order in range(1, 4):
        acc[...] = jnp.zeros_like(acc)

        def step(s, carry):
            found = []
            for u in range(group):
                t = s * group + u
                block = tile_block[t]
                row = lax.div(block, side)
                col = block - row * side
                piece = term[:, pl.ds(pl.multiple_of(col * BS, BS), BS)]
                product = lax.dot_general(
                    piece,
                    parts[t],
                    (((1,), (1,)), ((), ())),
                    preferred_element_type=jnp.float32,
                )
                found.append((row, product))
            for row, product in found:
                place = pl.ds(pl.multiple_of(row * BS, BS), BS)
                acc[:, place] = acc[:, place] + product
            return carry

        lax.fori_loop(0, count // group, step, 0)
        new = (acc[...] * (-step_root) / order).astype(jnp.bfloat16)
        if order < 3:
            term[...] = new
            total[...] = total[...] + new.astype(jnp.float32)
        else:
            out[0] = (total[...] + new.astype(jnp.float32)).astype(jnp.bfloat16)


def per_device(n, walkers, left_factor, chol_tiles, tile_block, fields):
    _, orbital_count, occupied = walkers.shape
    tiles, vectors, area = chol_tiles.shape
    all_tiles = n * tiles
    vmem = pl.BlockSpec(memory_space=pltpu.VMEM)
    smem = pl.BlockSpec(memory_space=pltpu.SMEM)
    anywhere = pl.BlockSpec(memory_space=pl.ANY)
    turned = walkers.transpose(0, 2, 1)
    green = pl.pallas_call(
        functools.partial(build_kernel, 4),
        out_shape=jax.ShapeDtypeStruct((all_tiles, BS, BS), jnp.bfloat16),
        in_specs=[smem, vmem, vmem],
        out_specs=vmem,
        scratch_shapes=[pltpu.VMEM((orbital_count // BS, BS, occupied), jnp.bfloat16)],
        compiler_params=pltpu.CompilerParams(vmem_limit_bytes=32 * 2**20),
        name="build",
    )(tile_block, turned, left_factor)
    force_bias, returned = pl.pallas_call(
        functools.partial(exchange_kernel, n),
        out_shape=(
            jax.ShapeDtypeStruct((n, tiles * vectors), jnp.float32),
            jax.ShapeDtypeStruct((all_tiles, BS, BS), jnp.bfloat16),
        ),
        in_specs=[vmem, vmem, anywhere],
        out_specs=(vmem, anywhere),
        scratch_shapes=[
            pltpu.VMEM((tiles, vectors, area), jnp.bfloat16),
            pltpu.VMEM((tiles, n, BS, BS), jnp.bfloat16),
            pltpu.VMEM((tiles, n, BS, BS), jnp.bfloat16),
            pltpu.VMEM((BS * n, BS), jnp.float32),
            pltpu.VMEM((n, area), jnp.bfloat16),
            pltpu.VMEM((tiles, n, vectors), jnp.float32),
            pltpu.VMEM((tiles, n, vectors), jnp.float32),
            pltpu.SemaphoreType.DMA((tiles,)),
            pltpu.SemaphoreType.DMA,
            pltpu.SemaphoreType.DMA((tiles,)),
            pltpu.SemaphoreType.DMA,
            pltpu.SemaphoreType.DMA,
            pltpu.SemaphoreType.DMA((tiles,)),
        ],
        compiler_params=pltpu.CompilerParams(
            collective_id=0, has_side_effects=True, vmem_limit_bytes=48 * 2**20
        ),
        name="exchange",
    )(green, fields, chol_tiles)
    new_walkers = pl.pallas_call(
        functools.partial(propagate_kernel, 8),
        out_shape=jax.ShapeDtypeStruct(turned.shape, jnp.bfloat16),
        in_specs=[smem, vmem, vmem],
        out_specs=vmem,
        scratch_shapes=[
            pltpu.VMEM((occupied, orbital_count), jnp.bfloat16),
            pltpu.VMEM((occupied, orbital_count), jnp.float32),
            pltpu.VMEM((occupied, orbital_count), jnp.float32),
        ],
        compiler_params=pltpu.CompilerParams(vmem_limit_bytes=48 * 2**20),
        name="propagate",
    )(tile_block, returned, turned)
    return (force_bias, new_walkers.transpose(0, 2, 1))


def solution(mesh):
    in_specs = (
        P(("parts", "chol"), None, None),
        P(("parts", "chol"), None, None),
        P("chol", None, None),
        P(),
        P("parts", "chol"),
    )
    out_specs = (P("parts", "chol"), P(("parts", "chol"), None, None))
    return jax.shard_map(
        functools.partial(per_device, mesh.shape["chol"]),
        mesh=mesh,
        in_specs=in_specs,
        out_specs=out_specs,
        check_vma=False,
    )
```

```python
import functools

import jax
import jax.numpy as jnp
from jax import lax
from jax.experimental import pallas as pl
from jax.experimental.pallas import tpu as pltpu
from jax.sharding import PartitionSpec as P

BS = 128
MESH = pl.DeviceIdType.MESH

step_root = 0.25
CHUNK = 2048


def exchange_kernel(
    n,
    tile_block,
    turned_hbm,
    factor_hbm,
    fields,
    chol_hbm,
    bias_out,
    returned,
    chol,
    turned,
    factor,
    rows,
    cols,
    green,
    received,
    back,
    wide,
    flat,
    field_tiles,
    bias_tiles,
    in_sem,
    chol_sem,
    green_send,
    green_recv,
    back_send,
    back_recv,
    own_sem,
):
    me = lax.axis_index("chol")
    part = lax.axis_index("parts")
    tiles, vectors, area = chol.shape
    half = n // 2

    side = rows.shape[0]
    turned_copy = pltpu.make_async_copy(turned_hbm.at[0], turned, in_sem.at[0])
    factor_copy = pltpu.make_async_copy(factor_hbm.at[0], factor, in_sem.at[1])
    turned_copy.start()
    factor_copy.start()
    chol_copies = [
        pltpu.make_async_copy(chol_hbm.at[j], chol.at[j], chol_sem.at[j]) for j in range(tiles)
    ]
    for copy in chol_copies:
        copy.start()

    barrier = pltpu.get_barrier_semaphore()

    def greet(r, carry):
        pl.semaphore_signal(
            barrier, inc=1, device_id=(part, lax.rem(me + r, n)), device_id_type=MESH
        )
        return carry

    lax.fori_loop(1, n, greet, 0)

    for j in range(tiles):
        field_tiles[j] = fields[:, j * vectors : (j + 1) * vectors]

    turned_copy.wait()
    for r in range(side):
        rows[r] = turned[:, r * BS : (r + 1) * BS].T
    factor_copy.wait()
    for r in range(side):
        cols[r] = factor[:, r * BS : (r + 1) * BS]

    def build(t):
        block = tile_block[t]
        row = lax.div(block, side)
        col = block - row * side
        return jnp.dot(rows[row], cols[col], preferred_element_type=jnp.float32).astype(
            jnp.bfloat16
        )

    def send_green(j, owner):
        t = owner * tiles + j
        green[t] = build(t)
        pltpu.make_async_remote_copy(
            src_ref=green.at[t],
            dst_ref=received.at[j, me],
            send_sem=green_send,
            recv_sem=green_recv.at[j],
            device_id=(part, owner),
            device_id_type=MESH,
        ).start()

    pl.semaphore_wait(barrier, n - 1)

    def send_tile(j, carry):
        send_green(j, lax.rem(me + half, n))

        def pair(i, c):
            send_green(j, lax.rem(me + half + i, n))
            send_green(j, lax.rem(me + i, n))
            return c

        return lax.fori_loop(1, half, pair, carry)

    lax.fori_loop(0, tiles, send_tile, 0)
    for j in range(tiles):
        received[j, me] = build(me * tiles + j)

    def send_back(j, walker):
        pltpu.make_async_remote_copy(
            src_ref=back.at[j, walker],
            dst_ref=returned.at[me * tiles + j],
            send_sem=back_send,
            recv_sem=back_recv,
            device_id=(part, walker),
            device_id_type=MESH,
        ).start()

    def process(j, carry):
        arrived = received.at[j, pl.ds(0, n - 1)]
        pltpu.make_async_copy(arrived, arrived, green_recv.at[j]).wait()
        pltpu.make_async_copy(chol_hbm.at[j], chol.at[j], chol_sem.at[j]).wait()
        for w in range(n):
            wide[pl.ds(w, BS, stride=n), :] = received[j, w].astype(jnp.float32)
        for i in range(BS):
            flat[:, i * BS : (i + 1) * BS] = wide[i * n : (i + 1) * n, :].astype(jnp.bfloat16)

        bias = jnp.zeros((n, vectors), jnp.float32)
        for c in range(area // CHUNK):
            bias = bias + lax.dot_general(
                flat[:, c * CHUNK : (c + 1) * CHUNK],
                chol[j, :, c * CHUNK : (c + 1) * CHUNK],
                (((1,), (1,)), ((), ())),
                preferred_element_type=jnp.float32,
            )
        bias_tiles[j] = bias
        shifted = (field_tiles[j] + bias).astype(jnp.bfloat16)
        for c in range(area // CHUNK):
            piece = jnp.dot(
                shifted,
                chol[j, :, c * CHUNK : (c + 1) * CHUNK],
                preferred_element_type=jnp.float32,
            )
            for i in range(CHUNK // BS):
                base = (c * (CHUNK // BS) + i) * n
                wide[base : base + n, :] = piece[:, i * BS : (i + 1) * BS]
        for w in range(n):
            back[j, w] = wide[pl.ds(w, BS, stride=n), :].astype(jnp.bfloat16)

        send_back(j, lax.rem(me + half, n))

        def pair(i, c):
            send_back(j, lax.rem(me + half + i, n))
            send_back(j, lax.rem(me + i, n))
            return c

        lax.fori_loop(1, half, pair, 0)
        pltpu.make_async_copy(
            back.at[j, me], returned.at[me * tiles + j], own_sem.at[j]
        ).start()
        return carry

    lax.fori_loop(0, tiles, process, 0)

    for j in range(tiles):
        bias_out[:, j * vectors : (j + 1) * vectors] = bias_tiles[j]

    others = pl.ds(0, (n - 1) * tiles)
    pltpu.make_async_copy(green.at[others], green.at[others], green_send).wait()
    pltpu.make_async_copy(green.at[others], green.at[others], back_send).wait()
    for j in range(tiles):
        pltpu.make_async_copy(
            back.at[j, me], returned.at[me * tiles + j], own_sem.at[j]
        ).wait()
    pltpu.make_async_copy(returned.at[others], returned.at[others], back_recv).wait()


def propagate_kernel(
    group, tile_block, parts, walkers, bias, out, bias_out, paired, term, acc, total, bias_sem
):
    bias_copy = pltpu.make_async_copy(bias, bias_out, bias_sem)
    bias_copy.start()
    pairs = paired.shape[0]
    side = walkers.shape[2] // BS
    zero = jnp.zeros((BS, BS), jnp.bfloat16)

    def place_of(index):
        return pl.ds(pl.multiple_of(index * BS, BS), BS)

    def pair_up(s, carry):
        for u in range(group):
            q = s * group + u
            paired[q, :BS, :BS] = parts[2 * q]
            paired[q, :BS, BS:] = zero
            paired[q, BS:, :BS] = zero
            paired[q, BS:, BS:] = parts[2 * q + 1]
        return carry

    lax.fori_loop(0, pairs // group, pair_up, 0)
    term[...] = walkers[0]
    total[...] = walkers[0].astype(jnp.float32)
    for order in range(1, 4):
        acc[...] = jnp.zeros_like(acc)

        def step(s, carry):
            found = []
            for u in range(group):
                q = s * group + u
                places, pieces = [], []
                for t in (2 * q, 2 * q + 1):
                    block = tile_block[t]
                    row = lax.div(block, side)
                    places.append(place_of(row))
                    pieces.append(term[:, place_of(block - row * side)])
                product = lax.dot_general(
                    jnp.concatenate(pieces, axis=1),
                    paired[q],
                    (((1,), (1,)), ((), ())),
                    preferred_element_type=jnp.float32,
                )
                found.append((places, product))
            for places, product in found:
                acc[:, places[0]] = acc[:, places[0]] + product[:, :BS]
                acc[:, places[1]] = acc[:, places[1]] + product[:, BS:]
            return carry

        lax.fori_loop(0, pairs // group, step, 0)
        new = (acc[...] * (-step_root) / order).astype(jnp.bfloat16)
        if order < 3:
            term[...] = new
            total[...] = total[...] + new.astype(jnp.float32)
        else:
            out[0] = (total[...] + new.astype(jnp.float32)).astype(jnp.bfloat16)
    bias_copy.wait()


def per_device(n, walkers, left_factor, chol_tiles, tile_block, fields):
    _, orbital_count, occupied = walkers.shape
    tiles, vectors, area = chol_tiles.shape
    all_tiles = n * tiles
    vmem = pl.BlockSpec(memory_space=pltpu.VMEM)
    smem = pl.BlockSpec(memory_space=pltpu.SMEM)
    anywhere = pl.BlockSpec(memory_space=pl.ANY)
    turned = walkers.transpose(0, 2, 1)
    force_bias, returned = pl.pallas_call(
        functools.partial(exchange_kernel, n),
        out_shape=(
            jax.ShapeDtypeStruct((n, tiles * vectors), jnp.float32),
            jax.ShapeDtypeStruct((all_tiles, BS, BS), jnp.bfloat16),
        ),
        in_specs=[smem, anywhere, anywhere, vmem, anywhere],
        out_specs=(vmem, anywhere),
        scratch_shapes=[
            pltpu.VMEM((tiles, vectors, area), jnp.bfloat16),
            pltpu.VMEM((occupied, orbital_count), jnp.bfloat16),
            pltpu.VMEM((occupied, orbital_count), jnp.bfloat16),
            pltpu.VMEM((orbital_count // BS, BS, occupied), jnp.bfloat16),
            pltpu.VMEM((orbital_count // BS, occupied, BS), jnp.bfloat16),
            pltpu.VMEM((all_tiles, BS, BS), jnp.bfloat16),
            pltpu.VMEM((tiles, n, BS, BS), jnp.bfloat16),
            pltpu.VMEM((tiles, n, BS, BS), jnp.bfloat16),
            pltpu.VMEM((BS * n, BS), jnp.float32),
            pltpu.VMEM((n, area), jnp.bfloat16),
            pltpu.VMEM((tiles, n, vectors), jnp.float32),
            pltpu.VMEM((tiles, n, vectors), jnp.float32),
            pltpu.SemaphoreType.DMA((2,)),
            pltpu.SemaphoreType.DMA((tiles,)),
            pltpu.SemaphoreType.DMA,
            pltpu.SemaphoreType.DMA((tiles,)),
            pltpu.SemaphoreType.DMA,
            pltpu.SemaphoreType.DMA,
            pltpu.SemaphoreType.DMA((tiles,)),
        ],
        compiler_params=pltpu.CompilerParams(
            collective_id=0, has_side_effects=True, vmem_limit_bytes=48 * 2**20
        ),
        name="exchange",
    )(tile_block, turned, left_factor, fields, chol_tiles)
    new_walkers, force_bias = pl.pallas_call(
        functools.partial(propagate_kernel, 4),
        out_shape=(
            jax.ShapeDtypeStruct(turned.shape, jnp.bfloat16),
            jax.ShapeDtypeStruct(force_bias.shape, jnp.float32),
        ),
        in_specs=[smem, vmem, vmem, vmem],
        out_specs=(vmem, anywhere),
        scratch_shapes=[
            pltpu.VMEM((all_tiles // 2, 2 * BS, 2 * BS), jnp.bfloat16),
            pltpu.VMEM((occupied, orbital_count), jnp.bfloat16),
            pltpu.VMEM((occupied, orbital_count), jnp.float32),
            pltpu.VMEM((occupied, orbital_count), jnp.float32),
            pltpu.SemaphoreType.DMA,
        ],
        compiler_params=pltpu.CompilerParams(vmem_limit_bytes=48 * 2**20),
        name="propagate",
    )(tile_block, returned, turned, force_bias)
    return (force_bias, new_walkers.transpose(0, 2, 1))


def solution(mesh):
    in_specs = (
        P(("parts", "chol"), None, None),
        P(("parts", "chol"), None, None),
        P("chol", None, None),
        P(),
        P("parts", "chol"),
    )
    out_specs = (P("parts", "chol"), P(("parts", "chol"), None, None))
    return jax.shard_map(
        functools.partial(per_device, mesh.shape["chol"]),
        mesh=mesh,
        in_specs=in_specs,
        out_specs=out_specs,
        check_vma=False,
    )
```

```python
import functools

import jax
import jax.numpy as jnp
from jax import lax
from jax.experimental import pallas as pl
from jax.experimental.pallas import tpu as pltpu
from jax.sharding import PartitionSpec as P

BS = 128
MESH = pl.DeviceIdType.MESH

step_root = 0.25
CHUNK = 2048


def exchange_kernel(
    n,
    tile_block,
    turned_hbm,
    factor_hbm,
    fields,
    chol_hbm,
    bias_out,
    returned,
    chol,
    fields_here,
    rows,
    cols,
    green,
    received,
    back,
    wide,
    flat,
    field_tiles,
    bias_tiles,
    in_sem,
    chol_sem,
    green_send,
    green_recv,
    back_send,
    back_recv,
    own_sem,
):
    me = lax.axis_index("chol")
    part = lax.axis_index("parts")
    tiles, vectors, area = chol.shape
    half = n // 2

    side = rows.shape[0]
    for r in range(side):
        place = pl.ds(r * BS, BS)
        pltpu.make_async_copy(turned_hbm.at[0, :, place], rows.at[r], in_sem.at[0]).start()
        pltpu.make_async_copy(factor_hbm.at[0, :, place], cols.at[r], in_sem.at[1]).start()
    fields_copy = pltpu.make_async_copy(fields, fields_here, in_sem.at[2])
    fields_copy.start()
    chol_copies = [
        pltpu.make_async_copy(chol_hbm.at[j], chol.at[j], chol_sem.at[j]) for j in range(tiles)
    ]
    for copy in chol_copies:
        copy.start()

    barrier = pltpu.get_barrier_semaphore()

    def greet(r, carry):
        pl.semaphore_signal(
            barrier, inc=1, device_id=(part, lax.rem(me + r, n)), device_id_type=MESH
        )
        return carry

    lax.fori_loop(1, n, greet, 0)

    pltpu.make_async_copy(rows, rows, in_sem.at[0]).wait()
    pltpu.make_async_copy(cols, cols, in_sem.at[1]).wait()

    def build(t):
        block = tile_block[t]
        row = lax.div(block, side)
        col = block - row * side
        return lax.dot_general(
            rows[row],
            cols[col],
            (((0,), (0,)), ((), ())),
            preferred_element_type=jnp.float32,
        ).astype(jnp.bfloat16)

    def send_green(j, owner):
        t = owner * tiles + j
        green[t] = build(t)
        pltpu.make_async_remote_copy(
            src_ref=green.at[t],
            dst_ref=received.at[j, me],
            send_sem=green_send,
            recv_sem=green_recv.at[j],
            device_id=(part, owner),
            device_id_type=MESH,
        ).start()

    pl.semaphore_wait(barrier, n - 1)

    def send_tile(j, carry):
        send_green(j, lax.rem(me + half, n))

        def pair(i, c):
            send_green(j, lax.rem(me + half + i, n))
            send_green(j, lax.rem(me + i, n))
            return c

        return lax.fori_loop(1, half, pair, carry)

    lax.fori_loop(0, tiles, send_tile, 0)
    for j in range(tiles):
        received[j, me] = build(me * tiles + j)
    fields_copy.wait()
    for j in range(tiles):
        field_tiles[j] = fields_here[:, j * vectors : (j + 1) * vectors]

    def send_back(j, walker):
        pltpu.make_async_remote_copy(
            src_ref=back.at[j, walker],
            dst_ref=returned.at[me * tiles + j],
            send_sem=back_send,
            recv_sem=back_recv,
            device_id=(part, walker),
            device_id_type=MESH,
        ).start()

    def process(j, carry):
        arrived = received.at[j, pl.ds(0, n - 1)]
        pltpu.make_async_copy(arrived, arrived, green_recv.at[j]).wait()
        pltpu.make_async_copy(chol_hbm.at[j], chol.at[j], chol_sem.at[j]).wait()
        for w in range(n):
            wide[pl.ds(w, BS, stride=n), :] = received[j, w].astype(jnp.float32)
        for i in range(BS):
            flat[:, i * BS : (i + 1) * BS] = wide[i * n : (i + 1) * n, :].astype(jnp.bfloat16)

        bias = jnp.zeros((n, vectors), jnp.float32)
        for c in range(area // CHUNK):
            bias = bias + lax.dot_general(
                flat[:, c * CHUNK : (c + 1) * CHUNK],
                chol[j, :, c * CHUNK : (c + 1) * CHUNK],
                (((1,), (1,)), ((), ())),
                preferred_element_type=jnp.float32,
            )
        bias_tiles[j] = bias
        shifted = (field_tiles[j] + bias).astype(jnp.bfloat16)
        for c in range(area // CHUNK):
            piece = jnp.dot(
                shifted,
                chol[j, :, c * CHUNK : (c + 1) * CHUNK],
                preferred_element_type=jnp.float32,
            )
            for i in range(CHUNK // BS):
                base = (c * (CHUNK // BS) + i) * n
                wide[base : base + n, :] = piece[:, i * BS : (i + 1) * BS]
        for w in range(n):
            back[j, w] = wide[pl.ds(w, BS, stride=n), :].astype(jnp.bfloat16)

        send_back(j, lax.rem(me + half, n))

        def pair(i, c):
            send_back(j, lax.rem(me + half + i, n))
            send_back(j, lax.rem(me + i, n))
            return c

        lax.fori_loop(1, half, pair, 0)
        pltpu.make_async_copy(
            back.at[j, me], returned.at[me * tiles + j], own_sem.at[j]
        ).start()
        return carry

    lax.fori_loop(0, tiles, process, 0)

    for j in range(tiles):
        bias_out[:, j * vectors : (j + 1) * vectors] = bias_tiles[j]

    others = pl.ds(0, (n - 1) * tiles)
    pltpu.make_async_copy(green.at[others], green.at[others], green_send).wait()
    pltpu.make_async_copy(green.at[others], green.at[others], back_send).wait()
    for j in range(tiles):
        pltpu.make_async_copy(
            back.at[j, me], returned.at[me * tiles + j], own_sem.at[j]
        ).wait()
    pltpu.make_async_copy(returned.at[others], returned.at[others], back_recv).wait()


def propagate_kernel(
    group, tile_block, parts, walkers, bias, out, bias_out, term, acc, total, bias_sem, out_sem
):
    bias_copy = pltpu.make_async_copy(bias, bias_out, bias_sem)
    bias_copy.start()
    count = parts.shape[0]
    side = term.shape[0]
    for r in range(side):
        term[r] = walkers[0, :, r * BS : (r + 1) * BS]
    for order in range(1, 4):
        for r in range(side):
            acc[r] = jnp.zeros(acc.shape[1:], jnp.float32)

        def step(s, carry):
            for u in range(group):
                t = s * group + u
                block = tile_block[t]
                row = lax.div(block, side)
                col = block - row * side
                acc[row] = acc[row] + lax.dot_general(
                    term[col],
                    parts[t],
                    (((1,), (1,)), ((), ())),
                    preferred_element_type=jnp.float32,
                )
            return carry

        lax.fori_loop(0, count // group, step, 0)
        for r in range(side):
            new = (acc[r] * (-step_root) / order).astype(jnp.bfloat16)
            if order == 1:
                before = walkers[0, :, r * BS : (r + 1) * BS].astype(jnp.float32)
            else:
                before = total[r]
            after = before + new.astype(jnp.float32)
            if order < 3:
                term[r] = new
                total[r] = after
            else:
                term[r] = after.astype(jnp.bfloat16)
                pltpu.make_async_copy(
                    term.at[r], out.at[0, :, pl.ds(r * BS, BS)], out_sem
                ).start()
    pltpu.make_async_copy(term, term, out_sem).wait()
    bias_copy.wait()


def per_device(n, walkers, left_factor, chol_tiles, tile_block, fields):
    _, orbital_count, occupied = walkers.shape
    tiles, vectors, area = chol_tiles.shape
    all_tiles = n * tiles
    side = orbital_count // BS
    vmem = pl.BlockSpec(memory_space=pltpu.VMEM)
    smem = pl.BlockSpec(memory_space=pltpu.SMEM)
    hbm = pl.BlockSpec(memory_space=pltpu.HBM)
    anywhere = pl.BlockSpec(memory_space=pl.ANY)
    turned = walkers.transpose(0, 2, 1)
    force_bias, returned = pl.pallas_call(
        functools.partial(exchange_kernel, n),
        out_shape=(
            jax.ShapeDtypeStruct((n, tiles * vectors), jnp.float32),
            jax.ShapeDtypeStruct((all_tiles, BS, BS), jnp.bfloat16),
        ),
        in_specs=[smem, hbm, hbm, hbm, hbm],
        out_specs=(vmem, anywhere),
        scratch_shapes=[
            pltpu.VMEM((tiles, vectors, area), jnp.bfloat16),
            pltpu.VMEM((n, tiles * vectors), jnp.float32),
            pltpu.VMEM((side, occupied, BS), jnp.bfloat16),
            pltpu.VMEM((side, occupied, BS), jnp.bfloat16),
            pltpu.VMEM((all_tiles, BS, BS), jnp.bfloat16),
            pltpu.VMEM((tiles, n, BS, BS), jnp.bfloat16),
            pltpu.VMEM((tiles, n, BS, BS), jnp.bfloat16),
            pltpu.VMEM((BS * n, BS), jnp.float32),
            pltpu.VMEM((n, area), jnp.bfloat16),
            pltpu.VMEM((tiles, n, vectors), jnp.float32),
            pltpu.VMEM((tiles, n, vectors), jnp.float32),
            pltpu.SemaphoreType.DMA((3,)),
            pltpu.SemaphoreType.DMA((tiles,)),
            pltpu.SemaphoreType.DMA,
            pltpu.SemaphoreType.DMA((tiles,)),
            pltpu.SemaphoreType.DMA,
            pltpu.SemaphoreType.DMA,
            pltpu.SemaphoreType.DMA((tiles,)),
        ],
        compiler_params=pltpu.CompilerParams(
            collective_id=0, has_side_effects=True, vmem_limit_bytes=48 * 2**20
        ),
        name="exchange",
    )(tile_block, turned, left_factor, fields, chol_tiles)
    new_walkers, force_bias = pl.pallas_call(
        functools.partial(propagate_kernel, 16),
        out_shape=(
            jax.ShapeDtypeStruct(turned.shape, jnp.bfloat16),
            jax.ShapeDtypeStruct(force_bias.shape, jnp.float32),
        ),
        in_specs=[smem, vmem, vmem, vmem],
        out_specs=(hbm, hbm),
        scratch_shapes=[
            pltpu.VMEM((side, occupied, BS), jnp.bfloat16),
            pltpu.VMEM((side, occupied, BS), jnp.float32),
            pltpu.VMEM((side, occupied, BS), jnp.float32),
            pltpu.SemaphoreType.DMA,
            pltpu.SemaphoreType.DMA,
        ],
        compiler_params=pltpu.CompilerParams(vmem_limit_bytes=48 * 2**20),
        name="propagate",
    )(tile_block, returned, turned, force_bias)
    return (force_bias, new_walkers.transpose(0, 2, 1))


def solution(mesh):
    in_specs = (
        P(("parts", "chol"), None, None),
        P(("parts", "chol"), None, None),
        P("chol", None, None),
        P(),
        P("parts", "chol"),
    )
    out_specs = (P("parts", "chol"), P(("parts", "chol"), None, None))
    return jax.shard_map(
        functools.partial(per_device, mesh.shape["chol"]),
        mesh=mesh,
        in_specs=in_specs,
        out_specs=out_specs,
        check_vma=False,
    )
```

```python
import functools

import jax
import jax.numpy as jnp
from jax import lax
from jax.experimental import pallas as pl
from jax.experimental.pallas import tpu as pltpu
from jax.sharding import PartitionSpec as P

BS = 128
MESH = pl.DeviceIdType.MESH

step_root = 0.25
CHUNK = 2048
GROUP = 16


def exchange_kernel(
    n,
    tile_block,
    turned_hbm,
    factor_hbm,
    fields,
    chol_hbm,
    bias_out,
    returned,
    chol,
    fields_here,
    rows,
    cols,
    green,
    received,
    back,
    wide,
    flat,
    field_tiles,
    bias_tiles,
    bias_all,
    in_sem,
    chol_sem,
    green_send,
    green_recv,
    back_send,
    back_recv,
    own_sem,
):
    me = lax.axis_index("chol")
    part = lax.axis_index("parts")
    tiles, vectors, area = chol.shape
    half = n // 2

    side = rows.shape[0]
    for r in range(side):
        place = pl.ds(r * BS, BS)
        pltpu.make_async_copy(turned_hbm.at[0, :, place], rows.at[r], in_sem.at[0]).start()
        pltpu.make_async_copy(factor_hbm.at[0, :, place], cols.at[r], in_sem.at[1]).start()
    fields_copy = pltpu.make_async_copy(fields, fields_here, in_sem.at[2])
    fields_copy.start()
    chol_copies = [
        pltpu.make_async_copy(chol_hbm.at[j], chol.at[j], chol_sem.at[j]) for j in range(tiles)
    ]
    for copy in chol_copies:
        copy.start()

    barrier = pltpu.get_barrier_semaphore()

    def greet(r, carry):
        pl.semaphore_signal(
            barrier, inc=1, device_id=(part, lax.rem(me + r, n)), device_id_type=MESH
        )
        return carry

    lax.fori_loop(1, n, greet, 0)

    pltpu.make_async_copy(rows, rows, in_sem.at[0]).wait()
    pltpu.make_async_copy(cols, cols, in_sem.at[1]).wait()

    def build(t):
        block = tile_block[t]
        row = lax.div(block, side)
        col = block - row * side
        return lax.dot_general(
            rows[row],
            cols[col],
            (((0,), (0,)), ((), ())),
            preferred_element_type=jnp.float32,
        ).astype(jnp.bfloat16)

    def send_green(j, owner):
        t = owner * tiles + j
        green[t] = build(t)
        pltpu.make_async_remote_copy(
            src_ref=green.at[t],
            dst_ref=received.at[j, me],
            send_sem=green_send.at[j],
            recv_sem=green_recv.at[j],
            device_id=(part, owner),
            device_id_type=MESH,
        ).start()

    pl.semaphore_wait(barrier, n - 1)

    def send_tile(j, carry):
        send_green(j, lax.rem(me + half, n))

        def pair(i, c):
            send_green(j, lax.rem(me + half + i, n))
            send_green(j, lax.rem(me + i, n))
            return c

        return lax.fori_loop(1, half, pair, carry)

    def sent(j):
        others = pl.ds(0, n - 1)
        pltpu.make_async_copy(green.at[others], green.at[others], green_send.at[j]).wait()

    ahead = min(2, tiles)
    lax.fori_loop(0, ahead, send_tile, 0)
    for j in range(tiles):
        received[j, me] = build(me * tiles + j)
    fields_copy.wait()
    for j in range(tiles):
        field_tiles[j] = fields_here[:, j * vectors : (j + 1) * vectors]

    def send_back(j, walker):
        pltpu.make_async_remote_copy(
            src_ref=back.at[j, walker],
            dst_ref=returned.at[me * tiles + j],
            send_sem=back_send,
            recv_sem=back_recv,
            device_id=(part, walker),
            device_id_type=MESH,
        ).start()

    def process(j, carry):
        @pl.when(j + ahead < tiles)
        def _():
            sent(j)
            send_tile(j + ahead, 0)

        arrived = received.at[j, pl.ds(0, n - 1)]
        pltpu.make_async_copy(arrived, arrived, green_recv.at[j]).wait()
        pltpu.make_async_copy(chol_hbm.at[j], chol.at[j], chol_sem.at[j]).wait()
        for w in range(n):
            wide[pl.ds(w, BS, stride=n), :] = received[j, w].astype(jnp.float32)
        for i in range(BS):
            flat[:, i * BS : (i + 1) * BS] = wide[i * n : (i + 1) * n, :].astype(jnp.bfloat16)

        bias = jnp.zeros((n, vectors), jnp.float32)
        for c in range(area // CHUNK):
            bias = bias + lax.dot_general(
                flat[:, c * CHUNK : (c + 1) * CHUNK],
                chol[j, :, c * CHUNK : (c + 1) * CHUNK],
                (((1,), (1,)), ((), ())),
                preferred_element_type=jnp.float32,
            )
        bias_tiles[j] = bias
        shifted = (field_tiles[j] + bias).astype(jnp.bfloat16)
        for c in range(area // CHUNK):
            piece = jnp.dot(
                shifted,
                chol[j, :, c * CHUNK : (c + 1) * CHUNK],
                preferred_element_type=jnp.float32,
            )
            for i in range(CHUNK // BS):
                base = (c * (CHUNK // BS) + i) * n
                wide[base : base + n, :] = piece[:, i * BS : (i + 1) * BS]
        for w in range(n):
            back[j, w] = wide[pl.ds(w, BS, stride=n), :].astype(jnp.bfloat16)

        send_back(j, lax.rem(me + half, n))

        def pair(i, c):
            send_back(j, lax.rem(me + half + i, n))
            send_back(j, lax.rem(me + i, n))
            return c

        lax.fori_loop(1, half, pair, 0)
        pltpu.make_async_copy(
            back.at[j, me], returned.at[me * tiles + j], own_sem.at[j]
        ).start()
        return carry

    lax.fori_loop(0, tiles, process, 0)

    for j in range(tiles):
        bias_all[:, j * vectors : (j + 1) * vectors] = bias_tiles[j]
    bias_copy = pltpu.make_async_copy(bias_all, bias_out, in_sem.at[3])
    bias_copy.start()

    others = pl.ds(0, (n - 1) * tiles)
    bias_copy.wait()
    for j in range(max(tiles - ahead, 0), tiles):
        sent(j)
    pltpu.make_async_copy(green.at[others], green.at[others], back_send).wait()
    for j in range(tiles):
        pltpu.make_async_copy(
            back.at[j, me], returned.at[me * tiles + j], own_sem.at[j]
        ).wait()
    pltpu.make_async_copy(returned.at[others], returned.at[others], back_recv).wait()


def propagate_kernel(
    group,
    tile_block,
    parts_hbm,
    walkers_hbm,
    bias,
    out,
    bias_out,
    parts,
    first,
    term,
    acc,
    total,
    bias_sem,
    out_sem,
    in_sem,
    parts_sem,
):
    count = parts.shape[0]
    side = term.shape[0]

    def group_copy(s):
        place = pl.ds(s * group, group)
        return pltpu.make_async_copy(parts_hbm.at[place], parts.at[place], parts_sem.at[s])

    for r in range(side):
        pltpu.make_async_copy(
            walkers_hbm.at[0, :, pl.ds(r * BS, BS)], first.at[r], in_sem
        ).start()
    for s in range(count // group):
        group_copy(s).start()
    bias_copy = pltpu.make_async_copy(bias, bias_out, bias_sem)
    bias_copy.start()
    pltpu.make_async_copy(first, first, in_sem).wait()
    for order in range(1, 4):
        for r in range(side):
            acc[r] = jnp.zeros(acc.shape[1:], jnp.float32)

        source = first if order == 1 else term

        def step(s, carry):
            if order == 1:
                group_copy(s).wait()
            for u in range(group):
                t = s * group + u
                block = tile_block[t]
                row = lax.div(block, side)
                col = block - row * side
                acc[row] = acc[row] + lax.dot_general(
                    source[col],
                    parts[t],
                    (((1,), (1,)), ((), ())),
                    preferred_element_type=jnp.float32,
                )
            return carry

        lax.fori_loop(0, count // group, step, 0)
        for r in range(side):
            new = (acc[r] * (-step_root) / order).astype(jnp.bfloat16)
            if order == 1:
                before = first[r].astype(jnp.float32)
            else:
                before = total[r]
            after = before + new.astype(jnp.float32)
            if order < 3:
                term[r] = new
                total[r] = after
            else:
                term[r] = after.astype(jnp.bfloat16)
                pltpu.make_async_copy(
                    term.at[r], out.at[0, :, pl.ds(r * BS, BS)], out_sem
                ).start()
    pltpu.make_async_copy(term, term, out_sem).wait()
    bias_copy.wait()


def per_device(n, walkers, left_factor, chol_tiles, tile_block, fields):
    _, orbital_count, occupied = walkers.shape
    tiles, vectors, area = chol_tiles.shape
    all_tiles = n * tiles
    side = orbital_count // BS
    smem = pl.BlockSpec(memory_space=pltpu.SMEM)
    hbm = pl.BlockSpec(memory_space=pltpu.HBM)
    turned = walkers.transpose(0, 2, 1)
    force_bias, returned = pl.pallas_call(
        functools.partial(exchange_kernel, n),
        out_shape=(
            jax.ShapeDtypeStruct((n, tiles * vectors), jnp.float32),
            jax.ShapeDtypeStruct((all_tiles, BS, BS), jnp.bfloat16),
        ),
        in_specs=[smem, hbm, hbm, hbm, hbm],
        out_specs=(hbm, hbm),
        scratch_shapes=[
            pltpu.VMEM((tiles, vectors, area), jnp.bfloat16),
            pltpu.VMEM((n, tiles * vectors), jnp.float32),
            pltpu.VMEM((side, occupied, BS), jnp.bfloat16),
            pltpu.VMEM((side, occupied, BS), jnp.bfloat16),
            pltpu.VMEM((all_tiles, BS, BS), jnp.bfloat16),
            pltpu.VMEM((tiles, n, BS, BS), jnp.bfloat16),
            pltpu.VMEM((tiles, n, BS, BS), jnp.bfloat16),
            pltpu.VMEM((BS * n, BS), jnp.float32),
            pltpu.VMEM((n, area), jnp.bfloat16),
            pltpu.VMEM((tiles, n, vectors), jnp.float32),
            pltpu.VMEM((tiles, n, vectors), jnp.float32),
            pltpu.VMEM((n, tiles * vectors), jnp.float32),
            pltpu.SemaphoreType.DMA((4,)),
            pltpu.SemaphoreType.DMA((tiles,)),
            pltpu.SemaphoreType.DMA((tiles,)),
            pltpu.SemaphoreType.DMA((tiles,)),
            pltpu.SemaphoreType.DMA,
            pltpu.SemaphoreType.DMA,
            pltpu.SemaphoreType.DMA((tiles,)),
        ],
        compiler_params=pltpu.CompilerParams(
            collective_id=0, has_side_effects=True, vmem_limit_bytes=60 * 2**20
        ),
        name="exchange",
    )(tile_block, turned, left_factor, fields, chol_tiles)
    new_walkers, force_bias = pl.pallas_call(
        functools.partial(propagate_kernel, GROUP),
        out_shape=(
            jax.ShapeDtypeStruct(turned.shape, jnp.bfloat16),
            jax.ShapeDtypeStruct(force_bias.shape, jnp.float32),
        ),
        in_specs=[smem, hbm, hbm, hbm],
        out_specs=(hbm, hbm),
        scratch_shapes=[
            pltpu.VMEM((all_tiles, BS, BS), jnp.bfloat16),
            pltpu.VMEM((side, occupied, BS), jnp.bfloat16),
            pltpu.VMEM((side, occupied, BS), jnp.bfloat16),
            pltpu.VMEM((side, occupied, BS), jnp.float32),
            pltpu.VMEM((side, occupied, BS), jnp.float32),
            pltpu.SemaphoreType.DMA,
            pltpu.SemaphoreType.DMA,
            pltpu.SemaphoreType.DMA,
            pltpu.SemaphoreType.DMA((all_tiles // GROUP,)),
        ],
        compiler_params=pltpu.CompilerParams(vmem_limit_bytes=60 * 2**20),
        name="propagate",
    )(tile_block, returned, turned, force_bias)
    return (force_bias, new_walkers.transpose(0, 2, 1))


def solution(mesh):
    in_specs = (
        P(("parts", "chol"), None, None),
        P(("parts", "chol"), None, None),
        P("chol", None, None),
        P(),
        P("parts", "chol"),
    )
    out_specs = (P("parts", "chol"), P(("parts", "chol"), None, None))
    return jax.shard_map(
        functools.partial(per_device, mesh.shape["chol"]),
        mesh=mesh,
        in_specs=in_specs,
        out_specs=out_specs,
        check_vma=False,
    )
```

```python
import functools

import jax
import jax.numpy as jnp
from jax import lax
from jax.experimental import pallas as pl
from jax.experimental.pallas import tpu as pltpu
from jax.sharding import PartitionSpec as P

BS = 128
MESH = pl.DeviceIdType.MESH

step_root = 0.25
CHUNK = 2048
GROUP = 16
LIMIT = 63 * 2**20


def exchange_kernel(
    n,
    tile_block,
    turned_hbm,
    factor_hbm,
    fields,
    chol_hbm,
    bias_out,
    returned,
    rows,
    chol,
    fields_here,
    cols,
    green,
    received,
    back,
    wide,
    flat,
    field_tiles,
    bias_tiles,
    in_sem,
    chol_sem,
    green_send,
    green_recv,
    back_send,
    back_recv,
    own_sem,
):
    me = lax.axis_index("chol")
    part = lax.axis_index("parts")
    tiles, vectors, area = chol.shape
    half = n // 2

    side = rows.shape[0]
    for r in range(side):
        place = pl.ds(r * BS, BS)
        pltpu.make_async_copy(turned_hbm.at[0, :, place], rows.at[r], in_sem.at[0]).start()
        pltpu.make_async_copy(factor_hbm.at[0, :, place], cols.at[r], in_sem.at[1]).start()
    fields_copy = pltpu.make_async_copy(fields, fields_here, in_sem.at[2])
    fields_copy.start()
    chol_copies = [
        pltpu.make_async_copy(chol_hbm.at[j], chol.at[j], chol_sem.at[j]) for j in range(tiles)
    ]
    for copy in chol_copies:
        copy.start()

    barrier = pltpu.get_barrier_semaphore()

    def greet(r, carry):
        pl.semaphore_signal(
            barrier, inc=1, device_id=(part, lax.rem(me + r, n)), device_id_type=MESH
        )
        return carry

    lax.fori_loop(1, n, greet, 0)

    pltpu.make_async_copy(rows, rows, in_sem.at[0]).wait()
    pltpu.make_async_copy(cols, cols, in_sem.at[1]).wait()

    def build(t):
        block = tile_block[t]
        row = lax.div(block, side)
        col = block - row * side
        return lax.dot_general(
            rows[row],
            cols[col],
            (((0,), (0,)), ((), ())),
            preferred_element_type=jnp.float32,
        ).astype(jnp.bfloat16)

    def send_green(j, owner):
        t = owner * tiles + j
        green[t] = build(t)
        pltpu.make_async_remote_copy(
            src_ref=green.at[t],
            dst_ref=received.at[j, me],
            send_sem=green_send.at[j],
            recv_sem=green_recv.at[j],
            device_id=(part, owner),
            device_id_type=MESH,
        ).start()

    pl.semaphore_wait(barrier, n - 1)

    def send_tile(j, carry):
        send_green(j, lax.rem(me + half, n))

        def pair(i, c):
            send_green(j, lax.rem(me + half + i, n))
            send_green(j, lax.rem(me + i, n))
            return c

        return lax.fori_loop(1, half, pair, carry)

    def sent(j):
        others = pl.ds(0, n - 1)
        pltpu.make_async_copy(green.at[others], green.at[others], green_send.at[j]).wait()

    ahead = min(2, tiles)
    lax.fori_loop(0, ahead, send_tile, 0)
    for j in range(tiles):
        received[j, me] = build(me * tiles + j)
    fields_copy.wait()
    for j in range(tiles):
        field_tiles[j] = fields_here[:, j * vectors : (j + 1) * vectors]

    def send_back(j, walker):
        pltpu.make_async_remote_copy(
            src_ref=back.at[j, walker],
            dst_ref=returned.at[me * tiles + j],
            send_sem=back_send,
            recv_sem=back_recv,
            device_id=(part, walker),
            device_id_type=MESH,
        ).start()

    def process(j, carry):
        @pl.when(j + ahead < tiles)
        def _():
            sent(j)
            send_tile(j + ahead, 0)

        arrived = received.at[j, pl.ds(0, n - 1)]
        pltpu.make_async_copy(arrived, arrived, green_recv.at[j]).wait()
        pltpu.make_async_copy(chol_hbm.at[j], chol.at[j], chol_sem.at[j]).wait()
        for w in range(n):
            wide[pl.ds(w, BS, stride=n), :] = received[j, w].astype(jnp.float32)
        for i in range(BS):
            flat[:, i * BS : (i + 1) * BS] = wide[i * n : (i + 1) * n, :].astype(jnp.bfloat16)

        bias = jnp.zeros((n, vectors), jnp.float32)
        for c in range(area // CHUNK):
            bias = bias + lax.dot_general(
                flat[:, c * CHUNK : (c + 1) * CHUNK],
                chol[j, :, c * CHUNK : (c + 1) * CHUNK],
                (((1,), (1,)), ((), ())),
                preferred_element_type=jnp.float32,
            )
        bias_tiles[j] = bias
        shifted = (field_tiles[j] + bias).astype(jnp.bfloat16)
        for c in range(area // CHUNK):
            piece = jnp.dot(
                shifted,
                chol[j, :, c * CHUNK : (c + 1) * CHUNK],
                preferred_element_type=jnp.float32,
            )
            for i in range(CHUNK // BS):
                base = (c * (CHUNK // BS) + i) * n
                wide[base : base + n, :] = piece[:, i * BS : (i + 1) * BS]
        for w in range(n):
            back[j, w] = wide[pl.ds(w, BS, stride=n), :].astype(jnp.bfloat16)

        send_back(j, lax.rem(me + half, n))

        def pair(i, c):
            send_back(j, lax.rem(me + half + i, n))
            send_back(j, lax.rem(me + i, n))
            return c

        lax.fori_loop(1, half, pair, 0)
        pltpu.make_async_copy(
            back.at[j, me], returned.at[me * tiles + j], own_sem.at[j]
        ).start()
        return carry

    lax.fori_loop(0, tiles, process, 0)

    for j in range(tiles):
        bias_out[:, j * vectors : (j + 1) * vectors] = bias_tiles[j]

    others = pl.ds(0, (n - 1) * tiles)
    for j in range(max(tiles - ahead, 0), tiles):
        sent(j)
    pltpu.make_async_copy(green.at[others], green.at[others], back_send).wait()
    for j in range(tiles):
        pltpu.make_async_copy(
            back.at[j, me], returned.at[me * tiles + j], own_sem.at[j]
        ).wait()
    pltpu.make_async_copy(returned.at[others], returned.at[others], back_recv).wait()


def propagate_kernel(
    group, tile_block, parts, first, bias, out, bias_out, term, acc, total, bias_sem, out_sem
):
    count = parts.shape[0]
    side = term.shape[0]
    bias_copy = pltpu.make_async_copy(bias, bias_out, bias_sem)
    bias_copy.start()
    for order in range(1, 4):
        for r in range(side):
            acc[r] = jnp.zeros(acc.shape[1:], jnp.float32)

        source = first if order == 1 else term

        def step(s, carry):
            for u in range(group):
                t = s * group + u
                block = tile_block[t]
                row = lax.div(block, side)
                col = block - row * side
                acc[row] = acc[row] + lax.dot_general(
                    source[col],
                    parts[t],
                    (((1,), (1,)), ((), ())),
                    preferred_element_type=jnp.float32,
                )
            return carry

        lax.fori_loop(0, count // group, step, 0)
        for r in range(side):
            new = (acc[r] * (-step_root) / order).astype(jnp.bfloat16)
            if order == 1:
                before = first[r].astype(jnp.float32)
            else:
                before = total[r]
            after = before + new.astype(jnp.float32)
            if order < 3:
                term[r] = new
                total[r] = after
            else:
                term[r] = after.astype(jnp.bfloat16)
                pltpu.make_async_copy(
                    term.at[r], out.at[0, :, pl.ds(r * BS, BS)], out_sem
                ).start()
    pltpu.make_async_copy(term, term, out_sem).wait()
    bias_copy.wait()


def per_device(n, walkers, left_factor, chol_tiles, tile_block, fields):
    _, orbital_count, occupied = walkers.shape
    tiles, vectors, area = chol_tiles.shape
    all_tiles = n * tiles
    side = orbital_count // BS
    smem = pl.BlockSpec(memory_space=pltpu.SMEM)
    hbm = pl.BlockSpec(memory_space=pltpu.HBM)
    turned = walkers.transpose(0, 2, 1)
    held = 2 * (all_tiles * BS * BS + orbital_count * occupied)
    limit = LIMIT - held
    vmem = pl.BlockSpec(memory_space=pltpu.VMEM)
    force_bias, returned, blocks = pl.pallas_call(
        functools.partial(exchange_kernel, n),
        out_shape=(
            pltpu.VMEM((n, tiles * vectors), jnp.float32),
            pltpu.VMEM((all_tiles, BS, BS), jnp.bfloat16),
            pltpu.VMEM((side, occupied, BS), jnp.bfloat16),
        ),
        in_specs=[smem, hbm, hbm, hbm, hbm],
        out_specs=(vmem, vmem, vmem),
        scratch_shapes=[
            pltpu.VMEM((tiles, vectors, area), jnp.bfloat16),
            pltpu.VMEM((n, tiles * vectors), jnp.float32),
            pltpu.VMEM((side, occupied, BS), jnp.bfloat16),
            pltpu.VMEM((all_tiles, BS, BS), jnp.bfloat16),
            pltpu.VMEM((tiles, n, BS, BS), jnp.bfloat16),
            pltpu.VMEM((tiles, n, BS, BS), jnp.bfloat16),
            pltpu.VMEM((BS * n, BS), jnp.float32),
            pltpu.VMEM((n, area), jnp.bfloat16),
            pltpu.VMEM((tiles, n, vectors), jnp.float32),
            pltpu.VMEM((tiles, n, vectors), jnp.float32),
            pltpu.SemaphoreType.DMA((3,)),
            pltpu.SemaphoreType.DMA((tiles,)),
            pltpu.SemaphoreType.DMA((tiles,)),
            pltpu.SemaphoreType.DMA((tiles,)),
            pltpu.SemaphoreType.DMA,
            pltpu.SemaphoreType.DMA,
            pltpu.SemaphoreType.DMA((tiles,)),
        ],
        compiler_params=pltpu.CompilerParams(
            collective_id=0, has_side_effects=True, vmem_limit_bytes=limit
        ),
        name="exchange",
    )(tile_block, turned, left_factor, fields, chol_tiles)
    new_walkers, force_bias = pl.pallas_call(
        functools.partial(propagate_kernel, GROUP),
        out_shape=(
            jax.ShapeDtypeStruct(turned.shape, jnp.bfloat16),
            jax.ShapeDtypeStruct(force_bias.shape, jnp.float32),
        ),
        in_specs=[smem, vmem, vmem, vmem],
        out_specs=(hbm, hbm),
        scratch_shapes=[
            pltpu.VMEM((side, occupied, BS), jnp.bfloat16),
            pltpu.VMEM((side, occupied, BS), jnp.float32),
            pltpu.VMEM((side, occupied, BS), jnp.float32),
            pltpu.SemaphoreType.DMA,
            pltpu.SemaphoreType.DMA,
        ],
        compiler_params=pltpu.CompilerParams(vmem_limit_bytes=24 * 2**20),
        name="propagate",
    )(tile_block, returned, blocks, force_bias)
    return (force_bias, new_walkers.transpose(0, 2, 1))


def solution(mesh):
    in_specs = (
        P(("parts", "chol"), None, None),
        P(("parts", "chol"), None, None),
        P("chol", None, None),
        P(),
        P("parts", "chol"),
    )
    out_specs = (P("parts", "chol"), P(("parts", "chol"), None, None))
    return jax.shard_map(
        functools.partial(per_device, mesh.shape["chol"]),
        mesh=mesh,
        in_specs=in_specs,
        out_specs=out_specs,
        check_vma=False,
    )
```

```python
import functools

import jax
import jax.numpy as jnp
from jax import lax
from jax.experimental import pallas as pl
from jax.experimental.pallas import tpu as pltpu
from jax.sharding import PartitionSpec as P

BS = 128
MESH = pl.DeviceIdType.MESH

step_root = 0.25
CHUNK = 2048
GROUP = 32
LIMIT = 63 * 2**20


def exchange_kernel(
    n,
    tile_block,
    turned_hbm,
    factor_hbm,
    fields,
    chol_hbm,
    bias_out,
    returned,
    rows,
    chol,
    fields_here,
    cols,
    green,
    received,
    back,
    wide,
    flat,
    field_tiles,
    bias_tiles,
    in_sem,
    chol_sem,
    green_send,
    green_recv,
    back_send,
    back_recv,
    own_sem,
):
    me = lax.axis_index("chol")
    part = lax.axis_index("parts")
    tiles, vectors, area = chol.shape
    half = n // 2

    side = rows.shape[0]
    for r in range(side):
        place = pl.ds(r * BS, BS)
        pltpu.make_async_copy(turned_hbm.at[0, :, place], rows.at[r], in_sem.at[0]).start()
        pltpu.make_async_copy(factor_hbm.at[0, :, place], cols.at[r], in_sem.at[1]).start()
    fields_copy = pltpu.make_async_copy(fields, fields_here, in_sem.at[2])
    fields_copy.start()
    chol_copies = [
        pltpu.make_async_copy(chol_hbm.at[j], chol.at[j], chol_sem.at[j]) for j in range(tiles)
    ]
    for copy in chol_copies:
        copy.start()

    barrier = pltpu.get_barrier_semaphore()

    def greet(r, carry):
        pl.semaphore_signal(
            barrier, inc=1, device_id=(part, lax.rem(me + r, n)), device_id_type=MESH
        )
        return carry

    lax.fori_loop(1, n, greet, 0)

    pltpu.make_async_copy(rows, rows, in_sem.at[0]).wait()
    pltpu.make_async_copy(cols, cols, in_sem.at[1]).wait()

    def build(t):
        block = tile_block[t]
        row = lax.div(block, side)
        col = block - row * side
        return lax.dot_general(
            rows[row],
            cols[col],
            (((0,), (0,)), ((), ())),
            preferred_element_type=jnp.float32,
        ).astype(jnp.bfloat16)

    def send_green(j, owner):
        t = owner * tiles + j
        green[t] = build(t)
        pltpu.make_async_remote_copy(
            src_ref=green.at[t],
            dst_ref=received.at[j, me],
            send_sem=green_send.at[j],
            recv_sem=green_recv.at[j],
            device_id=(part, owner),
            device_id_type=MESH,
        ).start()

    pl.semaphore_wait(barrier, n - 1)

    def send_tile(j, carry):
        send_green(j, lax.rem(me + half, n))

        def pair(i, c):
            send_green(j, lax.rem(me + half + i, n))
            send_green(j, lax.rem(me + i, n))
            return c

        return lax.fori_loop(1, half, pair, carry)

    def sent(j):
        others = pl.ds(0, n - 1)
        pltpu.make_async_copy(green.at[others], green.at[others], green_send.at[j]).wait()

    ahead = min(1, tiles)
    lax.fori_loop(0, ahead, send_tile, 0)
    for j in range(tiles):
        received[j, me] = build(me * tiles + j)
    fields_copy.wait()
    for j in range(tiles):
        field_tiles[j] = fields_here[:, j * vectors : (j + 1) * vectors]

    def send_back(j, walker):
        pltpu.make_async_remote_copy(
            src_ref=back.at[j, walker],
            dst_ref=returned.at[me * tiles + j],
            send_sem=back_send,
            recv_sem=back_recv,
            device_id=(part, walker),
            device_id_type=MESH,
        ).start()

    def process(j, carry):
        @pl.when(j + ahead < tiles)
        def _():
            sent(j)
            send_tile(j + ahead, 0)

        arrived = received.at[j, pl.ds(0, n - 1)]
        pltpu.make_async_copy(arrived, arrived, green_recv.at[j]).wait()
        pltpu.make_async_copy(chol_hbm.at[j], chol.at[j], chol_sem.at[j]).wait()
        for w in range(n):
            wide[pl.ds(w, BS, stride=n), :] = received[j, w].astype(jnp.float32)
        for i in range(BS):
            flat[:, i * BS : (i + 1) * BS] = wide[i * n : (i + 1) * n, :].astype(jnp.bfloat16)

        bias = jnp.zeros((n, vectors), jnp.float32)
        for c in range(area // CHUNK):
            bias = bias + lax.dot_general(
                flat[:, c * CHUNK : (c + 1) * CHUNK],
                chol[j, :, c * CHUNK : (c + 1) * CHUNK],
                (((1,), (1,)), ((), ())),
                preferred_element_type=jnp.float32,
            )
        bias_tiles[j] = bias
        shifted = (field_tiles[j] + bias).astype(jnp.bfloat16)
        for c in range(area // CHUNK):
            piece = jnp.dot(
                shifted,
                chol[j, :, c * CHUNK : (c + 1) * CHUNK],
                preferred_element_type=jnp.float32,
            )
            for i in range(CHUNK // BS):
                base = (c * (CHUNK // BS) + i) * n
                wide[base : base + n, :] = piece[:, i * BS : (i + 1) * BS]
        for w in range(n):
            back[j, w] = wide[pl.ds(w, BS, stride=n), :].astype(jnp.bfloat16)

        send_back(j, lax.rem(me + half, n))

        def pair(i, c):
            send_back(j, lax.rem(me + half + i, n))
            send_back(j, lax.rem(me + i, n))
            return c

        lax.fori_loop(1, half, pair, 0)
        pltpu.make_async_copy(
            back.at[j, me], returned.at[me * tiles + j], own_sem.at[j]
        ).start()
        return carry

    lax.fori_loop(0, tiles, process, 0)

    for j in range(tiles):
        bias_out[:, j * vectors : (j + 1) * vectors] = bias_tiles[j]

    others = pl.ds(0, (n - 1) * tiles)
    for j in range(max(tiles - ahead, 0), tiles):
        sent(j)
    pltpu.make_async_copy(green.at[others], green.at[others], back_send).wait()
    for j in range(tiles):
        pltpu.make_async_copy(
            back.at[j, me], returned.at[me * tiles + j], own_sem.at[j]
        ).wait()
    pltpu.make_async_copy(returned.at[others], returned.at[others], back_recv).wait()


def propagate_kernel(
    group, tile_block, parts, first, bias, out, bias_out, term, acc, total, bias_sem, out_sem
):
    count = parts.shape[0]
    side = term.shape[0]
    bias_copy = pltpu.make_async_copy(bias, bias_out, bias_sem)
    bias_copy.start()
    for order in range(1, 4):
        for r in range(side):
            acc[r] = jnp.zeros(acc.shape[1:], jnp.float32)

        source = first if order == 1 else term

        def step(s, carry):
            for u in range(group):
                t = s * group + u
                block = tile_block[t]
                row = lax.div(block, side)
                col = block - row * side
                acc[row] = acc[row] + lax.dot_general(
                    source[col],
                    parts[t],
                    (((1,), (1,)), ((), ())),
                    preferred_element_type=jnp.float32,
                )
            return carry

        lax.fori_loop(0, count // group, step, 0)
        for r in range(side):
            new = (acc[r] * (-step_root) / order).astype(jnp.bfloat16)
            if order == 1:
                before = first[r].astype(jnp.float32)
            else:
                before = total[r]
            after = before + new.astype(jnp.float32)
            if order < 3:
                term[r] = new
                total[r] = after
            else:
                term[r] = after.astype(jnp.bfloat16)
                pltpu.make_async_copy(
                    term.at[r], out.at[0, :, pl.ds(r * BS, BS)], out_sem
                ).start()
    pltpu.make_async_copy(term, term, out_sem).wait()
    bias_copy.wait()


def per_device(n, walkers, left_factor, chol_tiles, tile_block, fields):
    _, orbital_count, occupied = walkers.shape
    tiles, vectors, area = chol_tiles.shape
    all_tiles = n * tiles
    side = orbital_count // BS
    smem = pl.BlockSpec(memory_space=pltpu.SMEM)
    hbm = pl.BlockSpec(memory_space=pltpu.HBM)
    turned = walkers.transpose(0, 2, 1)
    held = 2 * (all_tiles * BS * BS + orbital_count * occupied)
    limit = LIMIT - held
    vmem = pl.BlockSpec(memory_space=pltpu.VMEM)
    force_bias, returned, blocks = pl.pallas_call(
        functools.partial(exchange_kernel, n),
        out_shape=(
            pltpu.VMEM((n, tiles * vectors), jnp.float32),
            pltpu.VMEM((all_tiles, BS, BS), jnp.bfloat16),
            pltpu.VMEM((side, occupied, BS), jnp.bfloat16),
        ),
        in_specs=[smem, hbm, hbm, hbm, hbm],
        out_specs=(vmem, vmem, vmem),
        scratch_shapes=[
            pltpu.VMEM((tiles, vectors, area), jnp.bfloat16),
            pltpu.VMEM((n, tiles * vectors), jnp.float32),
            pltpu.VMEM((side, occupied, BS), jnp.bfloat16),
            pltpu.VMEM((all_tiles, BS, BS), jnp.bfloat16),
            pltpu.VMEM((tiles, n, BS, BS), jnp.bfloat16),
            pltpu.VMEM((tiles, n, BS, BS), jnp.bfloat16),
            pltpu.VMEM((BS * n, BS), jnp.float32),
            pltpu.VMEM((n, area), jnp.bfloat16),
            pltpu.VMEM((tiles, n, vectors), jnp.float32),
            pltpu.VMEM((tiles, n, vectors), jnp.float32),
            pltpu.SemaphoreType.DMA((3,)),
            pltpu.SemaphoreType.DMA((tiles,)),
            pltpu.SemaphoreType.DMA((tiles,)),
            pltpu.SemaphoreType.DMA((tiles,)),
            pltpu.SemaphoreType.DMA,
            pltpu.SemaphoreType.DMA,
            pltpu.SemaphoreType.DMA((tiles,)),
        ],
        compiler_params=pltpu.CompilerParams(
            collective_id=0, has_side_effects=True, vmem_limit_bytes=limit
        ),
        name="exchange",
    )(tile_block, turned, left_factor, fields, chol_tiles)
    new_walkers, force_bias = pl.pallas_call(
        functools.partial(propagate_kernel, GROUP),
        out_shape=(
            jax.ShapeDtypeStruct(turned.shape, jnp.bfloat16),
            jax.ShapeDtypeStruct(force_bias.shape, jnp.float32),
        ),
        in_specs=[smem, vmem, vmem, vmem],
        out_specs=(hbm, hbm),
        scratch_shapes=[
            pltpu.VMEM((side, occupied, BS), jnp.bfloat16),
            pltpu.VMEM((side, occupied, BS), jnp.float32),
            pltpu.VMEM((side, occupied, BS), jnp.float32),
            pltpu.SemaphoreType.DMA,
            pltpu.SemaphoreType.DMA,
        ],
        compiler_params=pltpu.CompilerParams(vmem_limit_bytes=24 * 2**20),
        name="propagate",
    )(tile_block, returned, blocks, force_bias)
    return (force_bias, new_walkers.transpose(0, 2, 1))


def solution(mesh):
    in_specs = (
        P(("parts", "chol"), None, None),
        P(("parts", "chol"), None, None),
        P("chol", None, None),
        P(),
        P("parts", "chol"),
    )
    out_specs = (P("parts", "chol"), P(("parts", "chol"), None, None))
    return jax.shard_map(
        functools.partial(per_device, mesh.shape["chol"]),
        mesh=mesh,
        in_specs=in_specs,
        out_specs=out_specs,
        check_vma=False,
    )
```
